256 devices in a mesh: section: 4 (over x_hi, core), seq: 64 (over y, z, x_lo).
Axes of the slice: x: 4 (x_hi: 2, x_lo: 2; x = x_hi * 2 + x_lo), y: 4, z: 8, core: 2. Of those that a mesh axis runs over, the one named last changes fastest.
Arguments:
- stream: bfloat16 [4, 18432, 2560], P('section', 'seq'), may hold values from -6 to 6
- query: bfloat16 [4, 18432, 2560], P('section', 'seq'), may hold values from -60 to 60
- short_key: bfloat16 [4, 2048, 2560], P('section', 'seq'), may hold values from -8 to 8
- short_value: bfloat16 [4, 2048, 2560], P('section', 'seq'), may hold values from -16 to 16
- short_out: bfloat16 [4, 2048, 2560], P('section', 'seq'), may hold values from -6 to 6
Outputs:
- output: bfloat16 [4, 18432, 2560], P('section', 'seq')
- bottleneck: bfloat16 [4, 2048, 2560], P('section', 'seq')
The draws below stay inside these ranges and needn't reach their ends.
All inputs are finite; a program needn't handle non-finite values.
Results may differ from the reference program's by a relative error of at most 0.0085.
Values may be sent and summed in bfloat16 or wider, within the bound.
No kernel may reach another device: no remote copies, remote signals or barrier semaphores. Data moves between devices by JAX's collectives and lax.ppermute only.
A program may use at most 128 MiB of HBM per device.

```python
import math
import jax
import jax.numpy as jnp
from jax import lax

HEADS = 20
HEAD = 128
TOK_DEV = 288
FEAT = 2560
TOKENS = 18432
SHORT = 2048
SECTIONS = 4
N_SEQ = 64


def base_keys(key):
    return jnp.clip(2.0 * jax.random.normal(jax.random.fold_in(key, 11), (SECTIONS, SHORT, HEADS * HEAD), jnp.float32), -8.0, 8.0)


def draw_query(key, part):
    key = jax.random.fold_in(key, 1)
    drawn = jnp.clip(jax.random.normal(key, (SECTIONS, TOKENS, HEADS * HEAD), jnp.float32), -4.0, 4.0)
    return drawn.astype(jnp.bfloat16)


def draw_short_key(key, part):
    shared = base_keys(key)
    return shared.astype(jnp.bfloat16)


def block_levels(key, dims, cuts, smallest, top_value):
    def one(position, shards_of):
        steps = jax.random.uniform(jax.random.fold_in(jax.random.fold_in(key, 6), position), (shards_of,), jnp.float32, smallest / len(cuts), top_value / len(cuts))
        return jnp.repeat(jnp.exp(steps), dims[position] // shards_of).reshape((-1,) + (1,) * (len(dims) - position - 1))

    factor_of = one(*cuts[0])
    for cut in cuts[1:]:
        factor_of = factor_of * one(*cut)
    return factor_of


def centred(stream_key, shape, scale, bound, shards=(), kind=jnp.bfloat16):
    values = scale * jax.random.normal(stream_key, shape, jnp.float32)
    if shards:
        values = values * block_levels(stream_key, shape, shards, -0.22, 0.18)
    return jnp.clip(values, -bound, bound).astype(kind)


def setup_inputs(seed: int = 0) -> dict:
    seeds = jax.random.split(jax.random.key(seed), 6)
    stream = centred(seeds[0], (SECTIONS, TOKENS, FEAT), 1.0, 6.0, ((0, 4), (1, 64)))
    query = draw_query(jax.random.fold_in(seeds[5], 71), 0)
    short_key = draw_short_key(jax.random.fold_in(seeds[5], 71), 0)
    short_value = centred(seeds[3], (SECTIONS, SHORT, FEAT), 3.0, 16.0, ((0, 4), (1, 64)))
    short_out = centred(seeds[4], (SECTIONS, SHORT, FEAT), 1.0, 6.0, ((0, 4), (1, 64)))
    return {"stream": stream, "query": query, "short_key": short_key, "short_value": short_value, "short_out": short_out}


def shorten(stream_rows):
    widened = stream_rows.astype(jnp.float32)
    width = widened.shape[1]
    padded = jnp.concatenate([jnp.zeros((8, width), jnp.float32), widened[:-8]], axis=0)
    return (padded.reshape(-1, 9, width).sum(axis=1) / 9.0).astype(jnp.bfloat16)

def attend_block(query_rows, first_row, keys, values):
    query_heads = query_rows.astype(jnp.float32).reshape(TOK_DEV, HEADS, HEAD)
    key_heads = keys.astype(jnp.float32).reshape(SHORT, HEADS, HEAD)
    value_heads = values.astype(jnp.float32).reshape(SHORT, HEADS, HEAD)
    score = jnp.einsum('rhd,khd->hrk', query_heads, key_heads) * (1.0 / math.sqrt(HEAD))
    query_pos = first_row + jnp.arange(TOK_DEV, dtype=jnp.int32)
    key_pos = jnp.arange(SHORT, dtype=jnp.int32)
    allowed = (9 * key_pos[None, :] <= query_pos[:, None])[None]
    score = jnp.where(allowed, score, -1e+30)
    row_top = lax.optimization_barrier(jnp.max(score, axis=-1, keepdims=True))
    expo = jnp.where(allowed, jnp.exp(score - row_top), 0.0)
    rounded = lax.optimization_barrier(expo.astype(jnp.bfloat16)).astype(jnp.float32)
    numer = jnp.einsum('hrk,khd->hrd', rounded, value_heads)
    result = numer / lax.optimization_barrier(jnp.sum(expo, axis=-1, keepdims=True))
    return result.transpose(1, 0, 2).reshape(TOK_DEV, HEADS * HEAD).astype(jnp.bfloat16)

def attend(query, keys, values):
    blocks = query.reshape(N_SEQ, TOK_DEV, HEADS * HEAD)
    first_rows = jnp.arange(N_SEQ, dtype=jnp.int32) * TOK_DEV
    result = lax.map(lambda pair: attend_block(pair[0], pair[1], keys, values), (blocks, first_rows))
    return result.reshape(TOKENS, HEADS * HEAD)

def reference(stream, query, short_key, short_value, short_out):
    pooled = lax.map(shorten, stream)
    bottleneck = jnp.roll(pooled, 1, axis=0)
    attn = lax.map(lambda triple: attend(triple[0], triple[1], triple[2]), (query, short_key, short_value))
    mirrored = jnp.roll(stream, SECTIONS // 2, axis=0)
    upsampled = jnp.repeat(short_out, 9, axis=1)
    output = (mirrored.astype(jnp.float32) + upsampled.astype(jnp.float32) + attn.astype(jnp.float32)).astype(jnp.bfloat16)
    return (output, bottleneck)
```

```python
import functools
import math

import jax
import jax.numpy as jnp
from jax import lax
from jax.experimental import pallas as pl
from jax.experimental.pallas import tpu as pltpu
from jax.sharding import PartitionSpec as P

HEADS = 20
HEAD = 128
NY, NZ, NX = 4, 8, 2
GROUP = HEADS // NY
PHASES = ((0, 3), (3, 2))
SCALE = math.log2(math.e) / math.sqrt(HEAD)
VMEM = 20 * 1024 * 1024


def seq_pairs(dy, dz, dx):
    pairs = []
    for y in range(NY):
        for z in range(NZ):
            for x in range(NX):
                to = (((y + dy) % NY) * NZ + (z + dz) % NZ) * NX + (x + dx) % NX
                pairs.append(((y * NZ + z) * NX + x, to))
    return pairs


def move(block, dy=0, dz=0, dx=0):
    return lax.ppermute(block, "seq", seq_pairs(dy, dz, dx))


def section_shift(block, by):
    count = lax.axis_size("section")
    return lax.ppermute(block, "section", [(i, (i + by) % count) for i in range(count)])


def after(value, *others):
    return lax.optimization_barrier((value,) + others)[0]


def pack_kernel(where_ref, key_ref, value_ref, *refs):
    out_refs, (keys, values, sems) = refs[:NY], refs[NY:]
    copies = [
        pltpu.make_async_copy(key_ref, keys, sems.at[0]),
        pltpu.make_async_copy(value_ref, values, sems.at[1]),
    ]
    for copy in copies:
        copy.start()
    for copy in copies:
        copy.wait()
    part = GROUP * HEAD
    for d in range(NY):
        group = lax.rem(where_ref[0] + d, NY)
        columns = pl.ds(pl.multiple_of(group * part, part), part)
        out_refs[d][0] = keys[:, columns]
        out_refs[d][1] = values[:, columns]


def pack(where, keys, values):
    piece = jax.ShapeDtypeStruct((2, keys.shape[0], GROUP * HEAD), jnp.bfloat16)
    return pl.pallas_call(
        pack_kernel,
        in_specs=[pl.BlockSpec(memory_space=pltpu.SMEM)] + [pl.BlockSpec(memory_space=pl.ANY)] * 2,
        out_specs=[pl.BlockSpec(memory_space=pltpu.VMEM)] * NY,
        out_shape=[piece] * NY,
        scratch_shapes=[
            pltpu.VMEM(keys.shape, jnp.bfloat16),
            pltpu.VMEM(values.shape, jnp.bfloat16),
            pltpu.SemaphoreType.DMA((2,)),
        ],
        compiler_params=pltpu.CompilerParams(vmem_limit_bytes=VMEM),
        cost_estimate=pl.CostEstimate(flops=0, bytes_accessed=8 * keys.size, transcendentals=0),
    )(where, keys, values)


def pool_kernel(rim_ref, rows_ref, out_ref):
    count, rows = out_ref.shape[0], rows_ref.shape[0]
    j = lax.broadcasted_iota(jnp.int32, (count, rows), 0)
    r = lax.broadcasted_iota(jnp.int32, (count, rows), 1)
    inside = ((r <= 9 * j) & (r >= 9 * j - 8)).astype(jnp.bfloat16)
    first = (lax.broadcasted_iota(jnp.int32, (count, 8), 0) == 0).astype(jnp.bfloat16)
    total = jnp.dot(inside, rows_ref[...], preferred_element_type=jnp.float32)
    total += jnp.dot(first, rim_ref[...], preferred_element_type=jnp.float32)
    out_ref[...] = (total / 9.0).astype(out_ref.dtype)


def pool(rim, rows):
    count, width = rows.shape[0] // 9, rows.shape[1]
    return pl.pallas_call(
        pool_kernel,
        out_shape=jax.ShapeDtypeStruct((count, width), jnp.bfloat16),
        compiler_params=pltpu.CompilerParams(vmem_limit_bytes=VMEM),
        cost_estimate=pl.CostEstimate(
            flops=2 * count * rows.size, bytes_accessed=2 * rows.size + 2 * count * width, transcendentals=0
        ),
    )(rim, rows)


def attend_kernel(n_kv, first, where_ref, *refs):
    q_refs, refs = refs[:NY], refs[NY:]
    kv_refs, refs = refs[:n_kv], refs[n_kv:]
    out_refs, (qs, ks, vs, ss) = refs[:NY], refs[NY:]
    y, z, xl = where_ref[0], where_ref[1], where_ref[2]
    rows, keys = qs.shape[1], ks.shape[1]
    ones = jnp.ones((keys, HEAD), jnp.bfloat16)
    base = (z * NX + xl) * rows
    for h in range(out_refs[0].shape[1] // HEAD):
        column = slice(h * HEAD, h * HEAD + HEAD)
        for d in range(NY):
            g = lax.rem(y + NY - d, NY)
            if d == 0:
                own = pl.ds(pl.multiple_of((y * GROUP + first + h) * HEAD, HEAD), HEAD)
                qs[g] = q_refs[d][:, own]
            else:
                qs[g] = q_refs[d][:, (first + h) * HEAD : (first + h + 1) * HEAD]
            for n, (shift, slots) in enumerate(KV_ORDER):
                zz = lax.rem(z + shift, NZ)
                for at, slot in enumerate(slots):
                    xx = xl if slot == 0 else 1 - xl
                    place = pl.ds(pl.multiple_of((zz * NX + xx) * 32, 32), 32)
                    ks[g, place, :] = kv_refs[n][d, 0, at * 32 : at * 32 + 32, column]
                    vs[g, place, :] = kv_refs[n][d, 1, at * 32 : at * 32 + 32, column]
        tops = [None] * NY
        for k in range(NY):
            q = qs[k:].reshape((NY - k) * rows, HEAD)
            s = lax.dot_general(q, ks[k], (((1,), (1,)), ((), ())), preferred_element_type=jnp.float32)
            for g in range(k, NY):
                part = s[(g - k) * rows : (g - k + 1) * rows]
                if k == g:
                    col = lax.broadcasted_iota(jnp.int32, part.shape, 1)
                    row = lax.broadcasted_iota(jnp.int32, part.shape, 0)
                    part = jnp.where(9 * col - row <= base, part, -1e30)
                ss[k, g * rows : (g + 1) * rows, :] = part
                here = jnp.max(part, axis=-1, keepdims=True)
                tops[g] = here if k == 0 else jnp.maximum(tops[g], here)
        sums = [jnp.zeros((rows, 2 * HEAD), jnp.float32) for _ in range(NY)]
        for k in range(NY):
            values = jnp.concatenate([vs[k], ones], axis=1)
            for g in range(k, NY):
                p = jnp.exp2((ss[k, g * rows : (g + 1) * rows, :] - tops[g]) * SCALE)
                sums[g] += jnp.dot(p.astype(jnp.bfloat16), values, preferred_element_type=jnp.float32)
        for g in range(NY):
            qs[g] = (sums[g][:, :HEAD] / sums[g][:, HEAD:]).astype(jnp.bfloat16)
        for d in range(NY):
            out_refs[d][:, column] = qs[lax.rem(y + NY - d, NY)]


KV_ORDER = (
    (0, (0, 1)), (7, (0, 1)), (1, (0, 1)), (6, (0, 1)), (2, (0, 1)), (5, (0, 1)), (3, (0, 1)), (4, (0,)), (4, (1,)),
)


def attend(where, query, q_slots, arrivals, first, count):
    rows = query.shape[0]
    keys = NZ * NX * 32
    pairs = NY * (NY + 1) // 2 * rows * keys * count
    n_in = NY + len(arrivals)
    return pl.pallas_call(
        functools.partial(attend_kernel, len(arrivals), first),
        in_specs=[pl.BlockSpec(memory_space=pltpu.SMEM)] + [pl.BlockSpec(memory_space=pltpu.VMEM)] * n_in,
        out_specs=[pl.BlockSpec(memory_space=pltpu.VMEM)] * NY,
        out_shape=[jax.ShapeDtypeStruct((rows, count * HEAD), jnp.bfloat16)] * NY,
        scratch_shapes=[
            pltpu.VMEM((NY, rows, HEAD), jnp.bfloat16),
            pltpu.VMEM((NY, keys, HEAD), jnp.bfloat16),
            pltpu.VMEM((NY, keys, HEAD), jnp.bfloat16),
            pltpu.VMEM((NY, NY * rows, keys), jnp.float32),
        ],
        compiler_params=pltpu.CompilerParams(vmem_limit_bytes=VMEM),
        cost_estimate=pl.CostEstimate(
            flops=6 * pairs * HEAD, bytes_accessed=4 * NY * keys * HEAD * count, transcendentals=pairs
        ),
    )(where, query, *q_slots, *arrivals)


def finish_kernel(where_ref, mirrored_ref, short_ref, *refs):
    o_refs, out_ref = refs[:-1], refs[-1]
    y = where_ref[0]
    rows, count = out_ref.shape[0], short_ref.shape[0]
    i = lax.broadcasted_iota(jnp.int32, (rows, count), 0)
    j = lax.broadcasted_iota(jnp.int32, (rows, count), 1)
    spread = ((i >= 9 * j) & (i < 9 * j + 9)).astype(jnp.bfloat16)
    n = 0
    for first, heads in PHASES:
        for d in range(NY):
            g = lax.rem(y + d, NY)
            columns = pl.ds(pl.multiple_of((g * GROUP + first) * HEAD, HEAD), heads * HEAD)
            total = jnp.dot(spread, short_ref[:, columns], preferred_element_type=jnp.float32)
            total = mirrored_ref[:, columns].astype(jnp.float32) + total
            out_ref[:, columns] = (total + o_refs[n][...].astype(jnp.float32)).astype(out_ref.dtype)
            n += 1


def finish(where, mirrored, short_rows, o_slots):
    in_specs = [pl.BlockSpec(memory_space=pltpu.SMEM)]
    in_specs += [pl.BlockSpec(memory_space=pltpu.VMEM)] * (2 + len(o_slots))
    return pl.pallas_call(
        finish_kernel,
        in_specs=in_specs,
        out_shape=jax.ShapeDtypeStruct(mirrored.shape, jnp.bfloat16),
        compiler_params=pltpu.CompilerParams(vmem_limit_bytes=VMEM),
        cost_estimate=pl.CostEstimate(
            flops=4 * mirrored.size, bytes_accessed=6 * mirrored.size, transcendentals=0
        ),
    )(where, mirrored, short_rows, *o_slots)


def ring_step(step, ahead, back):
    if step == 4:
        half = ahead.shape[2] // 2
        ahead, back = ahead[:, :, :half], back[:, :, half:]
    return [move(ahead, dz=1), move(back, dz=-1)]


def ring(block):
    out = [block]
    for step in range(1, 5):
        out += ring_step(step, *(out[-2:] if step > 1 else [block, block]))
    return out


def body(stream, query, short_key, short_value, short_out):
    stream_rows, query_rows = stream[0], query[0]
    rows, width = stream_rows.shape
    seq = lax.axis_index("seq")
    y, z, xl = seq // (NZ * NX), seq // NX % NZ, seq % NX
    where = jnp.stack([y, z, xl]).astype(jnp.int32)
    part = GROUP * HEAD

    pieces = pack(where, short_key[0], short_value[0])
    own = [pieces[0]] + [move(pieces[d], dy=d) for d in range(1, NY)]
    other = [move(pieces[d], dy=d, dx=1) for d in range(NY)]
    block = jnp.concatenate([jnp.stack(own), jnp.stack(other)], axis=2)
    gathered = [ring(block[..., first * HEAD : (first + heads) * HEAD]) for first, heads in PHASES]

    query_late = after(query_rows, *own[1:], *other)
    q_slots = [
        move(lax.dynamic_slice_in_dim(query_late, (y + d) % NY * part, part, 1), dy=d)
        for d in range(1, NY)
    ]
    late_rows = after(stream_rows, *own[1:], *other)
    mirrored = section_shift(late_rows, 2)
    rim = lax.ppermute(late_rows[rows - 8 :], "seq", [(i, i + 1) for i in range(NY * NZ * NX - 1)])
    bottleneck = section_shift(pool(rim, stream_rows), 1)

    o_slots, before = [], []
    for (first, heads), arrivals in zip(PHASES, gathered):
        arrivals = [after(arrivals[0], *before)] + arrivals[1:]
        results = attend(where, query_rows, q_slots, arrivals, first, heads)
        before = results[:1]
        o_slots += [results[0]] + [move(results[d], dy=-d) for d in range(1, NY)]
    output = finish(where, mirrored, short_out[0], o_slots)
    return (output[None], bottleneck[None])


def solution(mesh):
    spec = P("section", "seq", None)
    return jax.shard_map(
        body, mesh=mesh, in_specs=(spec,) * 5, out_specs=(spec, spec), check_vma=False
    )
```

```python
import functools
import math

import jax
import jax.numpy as jnp
from jax import lax
from jax.experimental import pallas as pl
from jax.experimental.pallas import tpu as pltpu
from jax.sharding import PartitionSpec as P

HEADS = 20
HEAD = 128
NY, NZ, NX = 4, 8, 2
GROUP = HEADS // NY
PHASES = ((0, 3), (3, 2))
SCALE = math.log2(math.e) / math.sqrt(HEAD)
VMEM = 20 * 1024 * 1024


def seq_pairs(dy, dz, dx):
    pairs = []
    for y in range(NY):
        for z in range(NZ):
            for x in range(NX):
                to = (((y + dy) % NY) * NZ + (z + dz) % NZ) * NX + (x + dx) % NX
                pairs.append(((y * NZ + z) * NX + x, to))
    return pairs


def move(block, dy=0, dz=0, dx=0):
    return lax.ppermute(block, "seq", seq_pairs(dy, dz, dx))


def section_shift(block, by):
    count = lax.axis_size("section")
    return lax.ppermute(block, "section", [(i, (i + by) % count) for i in range(count)])


def after(value, *others):
    return lax.optimization_barrier((value,) + others)[0]


def pack_kernel(where_ref, key_ref, value_ref, *out_refs):
    part = GROUP * HEAD
    for d in range(NY):
        group = lax.rem(where_ref[0] + d, NY)
        columns = pl.ds(pl.multiple_of(group * part, part), part)
        out_refs[d][0] = key_ref[:, columns]
        out_refs[d][1] = value_ref[:, columns]


def pack(where, keys, values):
    piece = jax.ShapeDtypeStruct((2, keys.shape[0], GROUP * HEAD), jnp.bfloat16)
    return pl.pallas_call(
        pack_kernel,
        in_specs=[pl.BlockSpec(memory_space=pltpu.SMEM)] + [pl.BlockSpec(memory_space=pltpu.VMEM)] * 2,
        out_specs=[pl.BlockSpec(memory_space=pltpu.VMEM)] * NY,
        out_shape=[piece] * NY,
        compiler_params=pltpu.CompilerParams(vmem_limit_bytes=VMEM),
        cost_estimate=pl.CostEstimate(flops=0, bytes_accessed=8 * keys.size, transcendentals=0),
    )(where, keys, values)


def pool_kernel(rim_ref, rows_ref, out_ref):
    count, rows = out_ref.shape[0], rows_ref.shape[0]
    j = lax.broadcasted_iota(jnp.int32, (count, rows), 0)
    r = lax.broadcasted_iota(jnp.int32, (count, rows), 1)
    inside = ((r <= 9 * j) & (r >= 9 * j - 8)).astype(jnp.bfloat16)
    first = (lax.broadcasted_iota(jnp.int32, (count, 8), 0) == 0).astype(jnp.bfloat16)
    total = jnp.dot(inside, rows_ref[...], preferred_element_type=jnp.float32)
    total += jnp.dot(first, rim_ref[...], preferred_element_type=jnp.float32)
    out_ref[...] = (total / 9.0).astype(out_ref.dtype)


def pool(rim, rows):
    count, width = rows.shape[0] // 9, rows.shape[1]
    return pl.pallas_call(
        pool_kernel,
        out_shape=jax.ShapeDtypeStruct((count, width), jnp.bfloat16),
        compiler_params=pltpu.CompilerParams(vmem_limit_bytes=VMEM),
        cost_estimate=pl.CostEstimate(
            flops=2 * count * rows.size, bytes_accessed=2 * rows.size + 2 * count * width, transcendentals=0
        ),
    )(rim, rows)


def attend_kernel(n_kv, first, where_ref, *refs):
    q_refs, refs = refs[:NY], refs[NY:]
    kv_refs, refs = refs[:n_kv], refs[n_kv:]
    out_refs, (qs, ks, vs, ss) = refs[:NY], refs[NY:]
    y, z, xl = where_ref[0], where_ref[1], where_ref[2]
    rows, keys = qs.shape[1], ks.shape[1]
    ones = jnp.ones((keys, HEAD), jnp.bfloat16)
    base = (z * NX + xl) * rows
    for h in range(out_refs[0].shape[1] // HEAD):
        for d in range(NY):
            g = lax.rem(y + NY - d, NY)
            if d == 0:
                own = pl.ds(pl.multiple_of((y * GROUP + first + h) * HEAD, HEAD), HEAD)
                qs[g] = q_refs[d][:, own]
            else:
                qs[g] = q_refs[d][:, (first + h) * HEAD : (first + h + 1) * HEAD]
            for n, (shift, slots) in enumerate(KV_ORDER):
                zz = lax.rem(z + shift, NZ)
                at_head = first + h if kv_refs[n].shape[-1] == GROUP * HEAD else h
                column = slice(at_head * HEAD, at_head * HEAD + HEAD)
                for at, slot in enumerate(slots):
                    xx = xl if slot == 0 else 1 - xl
                    place = pl.ds(pl.multiple_of((zz * NX + xx) * 32, 32), 32)
                    ks[g, place, :] = kv_refs[n][d, 0, at * 32 : at * 32 + 32, column]
                    vs[g, place, :] = kv_refs[n][d, 1, at * 32 : at * 32 + 32, column]
        tops = [None] * NY
        for k in range(NY):
            q = qs[k:].reshape((NY - k) * rows, HEAD)
            s = lax.dot_general(q, ks[k], (((1,), (1,)), ((), ())), preferred_element_type=jnp.float32)
            for g in range(k, NY):
                part = s[(g - k) * rows : (g - k + 1) * rows]
                if k == g:
                    col = lax.broadcasted_iota(jnp.int32, part.shape, 1)
                    row = lax.broadcasted_iota(jnp.int32, part.shape, 0)
                    part = jnp.where(9 * col - row <= base, part, -1e30)
                ss[k, g * rows : (g + 1) * rows, :] = part
                here = jnp.max(part, axis=-1, keepdims=True)
                tops[g] = here if k == 0 else jnp.maximum(tops[g], here)
        sums = [jnp.zeros((rows, 2 * HEAD), jnp.float32) for _ in range(NY)]
        for k in range(NY):
            values = jnp.concatenate([vs[k], ones], axis=1)
            for g in range(k, NY):
                p = jnp.exp2((ss[k, g * rows : (g + 1) * rows, :] - tops[g]) * SCALE)
                sums[g] += jnp.dot(p.astype(jnp.bfloat16), values, preferred_element_type=jnp.float32)
        for g in range(NY):
            qs[g] = (sums[g][:, :HEAD] / sums[g][:, HEAD:]).astype(jnp.bfloat16)
        for d in range(NY):
            out_refs[d][:, h * HEAD : h * HEAD + HEAD] = qs[lax.rem(y + NY - d, NY)]


KV_ORDER = (
    (0, (0, 1)), (7, (0, 1)), (1, (0, 1)), (6, (0, 1)), (2, (0, 1)), (5, (0, 1)), (3, (0, 1)), (4, (0,)), (4, (1,)),
)


def attend(where, query, q_slots, arrivals, first, count):
    rows = query.shape[0]
    keys = NZ * NX * 32
    pairs = NY * (NY + 1) // 2 * rows * keys * count
    n_in = NY + len(arrivals)
    return pl.pallas_call(
        functools.partial(attend_kernel, len(arrivals), first),
        in_specs=[pl.BlockSpec(memory_space=pltpu.SMEM)] + [pl.BlockSpec(memory_space=pltpu.VMEM)] * n_in,
        out_specs=[pl.BlockSpec(memory_space=pltpu.VMEM)] * NY,
        out_shape=[jax.ShapeDtypeStruct((rows, count * HEAD), jnp.bfloat16)] * NY,
        scratch_shapes=[
            pltpu.VMEM((NY, rows, HEAD), jnp.bfloat16),
            pltpu.VMEM((NY, keys, HEAD), jnp.bfloat16),
            pltpu.VMEM((NY, keys, HEAD), jnp.bfloat16),
            pltpu.VMEM((NY, NY * rows, keys), jnp.float32),
        ],
        compiler_params=pltpu.CompilerParams(vmem_limit_bytes=VMEM),
        cost_estimate=pl.CostEstimate(
            flops=6 * pairs * HEAD, bytes_accessed=4 * NY * keys * HEAD * count, transcendentals=pairs
        ),
    )(where, query, *q_slots, *arrivals)


def base_kernel(mirrored_ref, short_ref, out_ref):
    rows, count = out_ref.shape[0], short_ref.shape[0]
    i = lax.broadcasted_iota(jnp.int32, (rows, count), 0)
    j = lax.broadcasted_iota(jnp.int32, (rows, count), 1)
    spread = ((i >= 9 * j) & (i < 9 * j + 9)).astype(jnp.bfloat16)
    total = jnp.dot(spread, short_ref[...], preferred_element_type=jnp.float32)
    out_ref[...] = mirrored_ref[...].astype(jnp.float32) + total


def base(mirrored, short_rows):
    return pl.pallas_call(
        base_kernel,
        in_specs=[pl.BlockSpec(memory_space=pltpu.VMEM)] * 2,
        out_specs=pl.BlockSpec(memory_space=pltpu.VMEM),
        out_shape=jax.ShapeDtypeStruct(mirrored.shape, jnp.float32),
        compiler_params=pltpu.CompilerParams(vmem_limit_bytes=VMEM),
        cost_estimate=pl.CostEstimate(
            flops=2 * short_rows.shape[0] * mirrored.size, bytes_accessed=6 * mirrored.size, transcendentals=0
        ),
    )(mirrored, short_rows)


def finish_kernel(where_ref, base_ref, pooled_ref, *refs):
    o_refs, (out_ref, bottle_ref, total, sems) = refs[:-4], refs[-4:]
    y, part = where_ref[0], GROUP * HEAD
    copies = [pltpu.make_async_copy(pooled_ref, bottle_ref, sems.at[NY])]
    copies[0].start()
    for d in range(NY):
        g = lax.rem(y + d, NY)
        for n, (first, heads) in enumerate(PHASES):
            columns = pl.ds(pl.multiple_of((g * GROUP + first) * HEAD, HEAD), heads * HEAD)
            summed = base_ref[:, columns] + o_refs[n * NY + d][...].astype(jnp.float32)
            total[:, columns] = summed.astype(out_ref.dtype)
        columns = pl.ds(pl.multiple_of(g * part, part), part)
        copies.append(pltpu.make_async_copy(total.at[:, columns], out_ref.at[:, columns], sems.at[d]))
        copies[-1].start()
    for copy in copies:
        copy.wait()


def finish(where, total, pooled, o_slots):
    in_specs = [pl.BlockSpec(memory_space=pltpu.SMEM)]
    in_specs += [pl.BlockSpec(memory_space=pltpu.VMEM)] * (2 + len(o_slots))
    return pl.pallas_call(
        finish_kernel,
        in_specs=in_specs,
        out_specs=[pl.BlockSpec(memory_space=pltpu.HBM)] * 2,
        out_shape=[
            jax.ShapeDtypeStruct(total.shape, jnp.bfloat16),
            jax.ShapeDtypeStruct(pooled.shape, jnp.bfloat16),
        ],
        scratch_shapes=[pltpu.VMEM(total.shape, jnp.bfloat16), pltpu.SemaphoreType.DMA((NY + 1,))],
        compiler_params=pltpu.CompilerParams(vmem_limit_bytes=VMEM),
        cost_estimate=pl.CostEstimate(flops=total.size, bytes_accessed=8 * total.size, transcendentals=0),
    )(where, total, pooled, *o_slots)


def ring_step(step, ahead, back):
    if step == 4:
        half = ahead.shape[2] // 2
        ahead, back = ahead[:, :, :half], back[:, :, half:]
    return [move(ahead, dz=1), move(back, dz=-1)]


def ring_steps(arrived, steps):
    for step in steps:
        arrived = arrived + ring_step(step, *(arrived[-2:] if step > 1 else arrived * 2))
    return arrived


def body(stream, query, short_key, short_value, short_out):
    stream_rows, query_rows = stream[0], query[0]
    rows = stream_rows.shape[0]
    seq = lax.axis_index("seq")
    y, z, xl = seq // (NZ * NX), seq // NX % NZ, seq % NX
    where = jnp.stack([y, z, xl]).astype(jnp.int32)
    part = GROUP * HEAD

    pieces = pack(where, short_key[0], short_value[0])
    own = [pieces[0]] + [move(pieces[d], dy=d) for d in range(1, NY)]
    other = [move(pieces[d], dy=d, dx=1) for d in range(NY)]
    block = jnp.concatenate([jnp.stack(own), jnp.stack(other)], axis=2)

    query_late = after(query_rows, block)
    q_slots = [
        move(lax.dynamic_slice_in_dim(query_late, (y + d) % NY * part, part, 1), dy=d)
        for d in range(1, NY)
    ]
    mirrored = section_shift(after(stream_rows, block), 2)

    def attended(phase, arrivals):
        results = attend(where, query_rows, q_slots, arrivals, *PHASES[phase])
        return results[0], [results[0]] + [move(results[d], dy=-d) for d in range(1, NY)]

    rim = lax.ppermute(
        after(stream_rows[rows - 8 :], block), "seq", [(i, i + 1) for i in range(NY * NZ * NX - 1)]
    )
    both = ring_steps([block], [1, 2])
    ends = [after(v, rim) for v in both[-2:]]
    a, b = [[v[..., first * HEAD : (first + heads) * HEAD] for v in ends] for first, heads in PHASES]
    a = both + ring_steps(a, [3, 4])[2:]
    b = both + ring_steps(b, [3])[2:]
    done, a_slots = attended(0, a)
    b = ring_steps([*b[:-2], *[after(v, done) for v in b[-2:]]], [4])
    pooled = pool(after(rim, done), stream_rows)
    done, b_slots = attended(1, [after(b[0], mirrored), *b[1:]])
    o_slots = a_slots + b_slots
    bottleneck = section_shift(after(pooled, done), 1)
    total = base(after(mirrored, done), short_out[0])
    output, bottleneck = finish(where, total, bottleneck, o_slots)
    return (output[None], bottleneck[None])


def solution(mesh):
    spec = P("section", "seq", None)
    return jax.shard_map(
        body, mesh=mesh, in_specs=(spec,) * 5, out_specs=(spec, spec), check_vma=False
    )
```

```python
import functools
import math

import jax
import jax.numpy as jnp
from jax import lax
from jax.experimental import pallas as pl
from jax.experimental.pallas import tpu as pltpu
from jax.sharding import PartitionSpec as P

HEADS = 20
HEAD = 128
NY, NZ, NX = 4, 8, 2
GROUP = HEADS // NY
PHASES = ((0, 3), (3, 2))
SCALE = math.log2(math.e) / math.sqrt(HEAD)
VMEM = 15 * 1024 * 1024


def seq_pairs(dy, dz, dx):
    pairs = []
    for y in range(NY):
        for z in range(NZ):
            for x in range(NX):
                to = (((y + dy) % NY) * NZ + (z + dz) % NZ) * NX + (x + dx) % NX
                pairs.append(((y * NZ + z) * NX + x, to))
    return pairs


def move(block, dy=0, dz=0, dx=0):
    return lax.ppermute(block, "seq", seq_pairs(dy, dz, dx))


def section_shift(block, by):
    count = lax.axis_size("section")
    return lax.ppermute(block, "section", [(i, (i + by) % count) for i in range(count)])


def next_rows(block):
    sections, count = lax.axis_size("section"), lax.axis_size("seq")
    pairs = [
        (s * count + i, (s + 1) % sections * count + i + 1) for s in range(sections) for i in range(count - 1)
    ]
    return lax.ppermute(block, ("section", "seq"), pairs)


def after(value, *others):
    return lax.optimization_barrier((value,) + others)[0]


def pack_kernel(where_ref, key_ref, value_ref, *out_refs):
    part = GROUP * HEAD
    for d in range(NY):
        group = lax.rem(where_ref[0] + d, NY)
        columns = pl.ds(pl.multiple_of(group * part, part), part)
        out_refs[d][0] = key_ref[:, columns]
        out_refs[d][1] = value_ref[:, columns]


def pack(where, keys, values):
    piece = jax.ShapeDtypeStruct((2, keys.shape[0], GROUP * HEAD), jnp.bfloat16)
    return pl.pallas_call(
        pack_kernel,
        in_specs=[pl.BlockSpec(memory_space=pltpu.SMEM)] + [pl.BlockSpec(memory_space=pltpu.VMEM)] * 2,
        out_specs=[pl.BlockSpec(memory_space=pltpu.VMEM)] * NY,
        out_shape=[piece] * NY,
        compiler_params=pltpu.CompilerParams(vmem_limit_bytes=VMEM),
        cost_estimate=pl.CostEstimate(flops=0, bytes_accessed=8 * keys.size, transcendentals=0),
    )(where, keys, values)


def pool_kernel(rows_ref, out_ref):
    count, rows = out_ref.shape[0], rows_ref.shape[0]
    j = lax.broadcasted_iota(jnp.int32, (count, rows), 0)
    r = lax.broadcasted_iota(jnp.int32, (count, rows), 1)
    inside = ((r <= 9 * j) & (r >= 9 * j - 8)).astype(jnp.bfloat16)
    total = jnp.dot(inside, rows_ref[...], preferred_element_type=jnp.float32)
    whole = lax.broadcasted_iota(jnp.int32, total.shape, 0) > 0
    out_ref[...] = jnp.where(whole, total / 9.0, total).astype(out_ref.dtype)


def pool(rows):
    count, width = rows.shape[0] // 9, rows.shape[1]
    return pl.pallas_call(
        pool_kernel,
        out_shape=jax.ShapeDtypeStruct((count, width), jnp.bfloat16),
        compiler_params=pltpu.CompilerParams(vmem_limit_bytes=VMEM),
        cost_estimate=pl.CostEstimate(
            flops=2 * count * rows.size, bytes_accessed=2 * rows.size + 2 * count * width, transcendentals=0
        ),
    )(rows)


def attend_kernel(n_kv, first, where_ref, *refs):
    q_refs, refs = refs[:NY], refs[NY:]
    kv_refs, refs = refs[:n_kv], refs[n_kv:]
    out_refs, (qs, ks, vs, ss) = refs[:NY], refs[NY:]
    y, z, xl = where_ref[0], where_ref[1], where_ref[2]
    rows, keys = qs.shape[1], ks.shape[1]
    ones = jnp.ones((keys, HEAD), jnp.bfloat16)
    base = (z * NX + xl) * rows
    for h in range(out_refs[0].shape[1] // HEAD):
        for d in range(NY):
            g = lax.rem(y + NY - d, NY)
            if d == 0:
                own = pl.ds(pl.multiple_of((y * GROUP + first + h) * HEAD, HEAD), HEAD)
                qs[g] = q_refs[d][:, own]
            else:
                qs[g] = q_refs[d][:, (first + h) * HEAD : (first + h + 1) * HEAD]
            for n, (shift, slots) in enumerate(KV_ORDER):
                zz = lax.rem(z + shift, NZ)
                at_head = first + h if kv_refs[n].shape[-1] == GROUP * HEAD else h
                column = slice(at_head * HEAD, at_head * HEAD + HEAD)
                for at, slot in enumerate(slots):
                    xx = xl if slot == 0 else 1 - xl
                    place = pl.ds(pl.multiple_of((zz * NX + xx) * 32, 32), 32)
                    ks[g, place, :] = kv_refs[n][d, 0, at * 32 : at * 32 + 32, column]
                    vs[g, place, :] = kv_refs[n][d, 1, at * 32 : at * 32 + 32, column]
        tops = [None] * NY
        for k in range(NY):
            q = qs[k:].reshape((NY - k) * rows, HEAD)
            s = lax.dot_general(q, ks[k], (((1,), (1,)), ((), ())), preferred_element_type=jnp.float32)
            for g in range(k, NY):
                part = s[(g - k) * rows : (g - k + 1) * rows]
                if k == g:
                    col = lax.broadcasted_iota(jnp.int32, part.shape, 1)
                    row = lax.broadcasted_iota(jnp.int32, part.shape, 0)
                    part = jnp.where(9 * col - row <= base, part, -1e30)
                ss[g * (g + 1) // 2 + k] = part
                here = jnp.max(part, axis=-1, keepdims=True)
                tops[g] = here if k == 0 else jnp.maximum(tops[g], here)
        sums = [jnp.zeros((rows, 2 * HEAD), jnp.float32) for _ in range(NY)]
        for k in range(NY):
            values = jnp.concatenate([vs[k], ones], axis=1)
            for g in range(k, NY):
                p = jnp.exp2((ss[g * (g + 1) // 2 + k] - tops[g]) * SCALE)
                sums[g] += jnp.dot(p.astype(jnp.bfloat16), values, preferred_element_type=jnp.float32)
        for g in range(NY):
            qs[g] = (sums[g][:, :HEAD] / sums[g][:, HEAD:]).astype(jnp.bfloat16)
        for d in range(NY):
            out_refs[d][:, h * HEAD : h * HEAD + HEAD] = qs[lax.rem(y + NY - d, NY)]


KV_ORDER = (
    (0, (0, 1)), (7, (0, 1)), (1, (0, 1)), (6, (0, 1)), (2, (0, 1)), (5, (0, 1)), (3, (0, 1)), (4, (0,)), (4, (1,)),
)


def attend(where, query, q_slots, arrivals, first, count):
    rows = query.shape[0]
    keys = NZ * NX * 32
    pairs = NY * (NY + 1) // 2 * rows * keys * count
    n_in = NY + len(arrivals)
    return pl.pallas_call(
        functools.partial(attend_kernel, len(arrivals), first),
        in_specs=[pl.BlockSpec(memory_space=pltpu.SMEM)] + [pl.BlockSpec(memory_space=pltpu.VMEM)] * n_in,
        out_specs=[pl.BlockSpec(memory_space=pltpu.VMEM)] * NY,
        out_shape=[jax.ShapeDtypeStruct((rows, count * HEAD), jnp.bfloat16)] * NY,
        scratch_shapes=[
            pltpu.VMEM((NY, rows, HEAD), jnp.bfloat16),
            pltpu.VMEM((NY, keys, HEAD), jnp.bfloat16),
            pltpu.VMEM((NY, keys, HEAD), jnp.bfloat16),
            pltpu.VMEM((NY * (NY + 1) // 2, rows, keys), jnp.float32),
        ],
        compiler_params=pltpu.CompilerParams(vmem_limit_bytes=VMEM),
        cost_estimate=pl.CostEstimate(
            flops=6 * pairs * HEAD, bytes_accessed=4 * NY * keys * HEAD * count, transcendentals=pairs
        ),
    )(where, query, *q_slots, *arrivals)


def base_kernel(mirrored_ref, short_ref, out_ref):
    rows, count = out_ref.shape[0], short_ref.shape[0]
    i = lax.broadcasted_iota(jnp.int32, (rows, count), 0)
    j = lax.broadcasted_iota(jnp.int32, (rows, count), 1)
    spread = ((i >= 9 * j) & (i < 9 * j + 9)).astype(jnp.bfloat16)
    total = jnp.dot(spread, short_ref[...], preferred_element_type=jnp.float32)
    out_ref[...] = mirrored_ref[...].astype(jnp.float32) + total


def base(mirrored, short_rows):
    return pl.pallas_call(
        base_kernel,
        in_specs=[pl.BlockSpec(memory_space=pltpu.VMEM)] * 2,
        out_specs=pl.BlockSpec(memory_space=pltpu.VMEM),
        out_shape=jax.ShapeDtypeStruct(mirrored.shape, jnp.float32),
        compiler_params=pltpu.CompilerParams(vmem_limit_bytes=VMEM),
        cost_estimate=pl.CostEstimate(
            flops=2 * short_rows.shape[0] * mirrored.size, bytes_accessed=6 * mirrored.size, transcendentals=0
        ),
    )(mirrored, short_rows)


def finish_kernel(where_ref, base_ref, pooled_ref, rim_ref, *refs):
    o_refs, (out_ref, bottle_ref, total, pooled, sems) = refs[:-5], refs[-5:]
    y, part = where_ref[0], GROUP * HEAD
    rows = pooled_ref[...].astype(jnp.float32)
    rim = jnp.sum(rim_ref[...].astype(jnp.float32), axis=0, keepdims=True)
    top = lax.broadcasted_iota(jnp.int32, rows.shape, 0) == 0
    pooled[...] = jnp.where(top, (rows + rim) / 9.0, rows).astype(pooled.dtype)
    copies = [pltpu.make_async_copy(pooled, bottle_ref, sems.at[NY])]
    copies[0].start()
    for d in range(NY):
        g = lax.rem(y + d, NY)
        for n, (first, heads) in enumerate(PHASES):
            columns = pl.ds(pl.multiple_of((g * GROUP + first) * HEAD, HEAD), heads * HEAD)
            summed = base_ref[:, columns] + o_refs[n * NY + d][...].astype(jnp.float32)
            total[:, columns] = summed.astype(out_ref.dtype)
        columns = pl.ds(pl.multiple_of(g * part, part), part)
        copies.append(pltpu.make_async_copy(total.at[:, columns], out_ref.at[:, columns], sems.at[d]))
        copies[-1].start()
    for copy in copies:
        copy.wait()


def finish(where, total, pooled, rim, o_slots):
    in_specs = [pl.BlockSpec(memory_space=pltpu.SMEM)]
    in_specs += [pl.BlockSpec(memory_space=pltpu.VMEM)] * (3 + len(o_slots))
    return pl.pallas_call(
        finish_kernel,
        in_specs=in_specs,
        out_specs=[pl.BlockSpec(memory_space=pltpu.HBM)] * 2,
        out_shape=[
            jax.ShapeDtypeStruct(total.shape, jnp.bfloat16),
            jax.ShapeDtypeStruct(pooled.shape, jnp.bfloat16),
        ],
        scratch_shapes=[
            pltpu.VMEM(total.shape, jnp.bfloat16),
            pltpu.VMEM(pooled.shape, jnp.bfloat16),
            pltpu.SemaphoreType.DMA((NY + 1,)),
        ],
        compiler_params=pltpu.CompilerParams(vmem_limit_bytes=VMEM),
        cost_estimate=pl.CostEstimate(flops=total.size, bytes_accessed=8 * total.size, transcendentals=0),
    )(where, total, pooled, rim, *o_slots)


def ring_step(step, ahead, back):
    if step == 4:
        half = ahead.shape[2] // 2
        ahead, back = ahead[:, :, :half], back[:, :, half:]
    return [move(ahead, dz=1), move(back, dz=-1)]


def ring_steps(arrived, steps):
    for step in steps:
        arrived = arrived + ring_step(step, *(arrived[-2:] if step > 1 else arrived * 2))
    return arrived


def body(stream, query, short_key, short_value, short_out):
    stream_rows, query_rows = stream[0], query[0]
    rows = stream_rows.shape[0]
    seq = lax.axis_index("seq")
    y, z, xl = seq // (NZ * NX), seq // NX % NZ, seq % NX
    where = jnp.stack([y, z, xl]).astype(jnp.int32)
    part = GROUP * HEAD

    pieces = pack(where, short_key[0], short_value[0])
    own = [pieces[0]] + [move(pieces[d], dy=d) for d in range(1, NY)]
    mine = jnp.stack(own)
    other = [move(after(pieces[d], own[1]), dy=d, dx=1) for d in range(NY)]
    others = jnp.stack(other)
    block = jnp.concatenate([mine, others], axis=2)

    query_late = after(query_rows, block)
    q_slots = [
        move(lax.dynamic_slice_in_dim(query_late, (y + d) % NY * part, part, 1), dy=d)
        for d in range(1, NY)
    ]
    mirrored = section_shift(after(stream_rows, block), 2)

    def attended(phase, arrivals):
        results = attend(where, query_rows, q_slots, arrivals, *PHASES[phase])
        return results[0], [results[0]] + [move(results[d], dy=-d) for d in range(1, NY)]

    first_in = [jnp.concatenate(pair, axis=2) for pair in zip(ring_step(1, mine, mine), ring_step(1, others, others))]
    pooled = pool(stream_rows)
    bottleneck = section_shift(after(pooled, mirrored), 1)
    rim = next_rows(after(stream_rows[rows - 8 :], mirrored))
    first_in = list(lax.optimization_barrier(tuple(first_in)))
    both = [block, *[after(v, q_slots[0]) for v in first_in]]
    both = ring_steps(both, [2])
    ends = [after(v, q_slots[2]) for v in both[-2:]]
    a, b = [[v[..., first * HEAD : (first + heads) * HEAD] for v in ends] for first, heads in PHASES]
    a = both + ring_steps(a, [3])[2:]
    a = ring_steps([*a[:-2], *[after(v, q_slots[1]) for v in a[-2:]]], [4])
    b = both + ring_steps(b, [3])[2:]
    done, a_slots = attended(0, [after(a[0], mirrored), *a[1:]])
    b = ring_steps([*b[:-2], *[after(v, done, rim, bottleneck) for v in b[-2:]]], [4])
    done, b_slots = attended(1, [after(b[0], mirrored), *b[1:]])
    o_slots = a_slots + b_slots
    total = base(after(mirrored, done), short_out[0])
    output, bottleneck = finish(where, total, bottleneck, rim, o_slots)
    return (output[None], bottleneck[None])


def solution(mesh):
    spec = P("section", "seq", None)
    return jax.shard_map(
        body, mesh=mesh, in_specs=(spec,) * 5, out_specs=(spec, spec), check_vma=False
    )
```

```python
import functools
import math

import jax
import jax.numpy as jnp
from jax import lax
from jax.experimental import pallas as pl
from jax.experimental.pallas import tpu as pltpu
from jax.sharding import PartitionSpec as P

HEADS = 20
HEAD = 128
NY, NZ, NX = 4, 8, 2
GROUP = HEADS // NY
PHASES = ((0, 3), (3, 2))
SCALE = math.log2(math.e) / math.sqrt(HEAD)
VMEM = 15 * 1024 * 1024


def seq_pairs(dy, dz, dx):
    pairs = []
    for y in range(NY):
        for z in range(NZ):
            for x in range(NX):
                to = (((y + dy) % NY) * NZ + (z + dz) % NZ) * NX + (x + dx) % NX
                pairs.append(((y * NZ + z) * NX + x, to))
    return pairs


def move(block, dy=0, dz=0, dx=0):
    return lax.ppermute(block, "seq", seq_pairs(dy, dz, dx))


def section_shift(block, by):
    count = lax.axis_size("section")
    return lax.ppermute(block, "section", [(i, (i + by) % count) for i in range(count)])


def next_rows(block):
    sections, count = lax.axis_size("section"), lax.axis_size("seq")
    pairs = [
        (s * count + i, (s + 1) % sections * count + i + 1) for s in range(sections) for i in range(count - 1)
    ]
    return lax.ppermute(block, ("section", "seq"), pairs)


def after(value, *others):
    return lax.optimization_barrier((value,) + others)[0]


def pack_kernel(where_ref, key_ref, value_ref, *out_refs):
    part = GROUP * HEAD
    for d in range(NY):
        group = lax.rem(where_ref[0] + d, NY)
        columns = pl.ds(pl.multiple_of(group * part, part), part)
        out_refs[d][0] = key_ref[:, columns]
        out_refs[d][1] = value_ref[:, columns]


def pack(where, keys, values):
    piece = jax.ShapeDtypeStruct((2, keys.shape[0], GROUP * HEAD), jnp.bfloat16)
    return pl.pallas_call(
        pack_kernel,
        in_specs=[pl.BlockSpec(memory_space=pltpu.SMEM)] + [pl.BlockSpec(memory_space=pltpu.VMEM)] * 2,
        out_specs=[pl.BlockSpec(memory_space=pltpu.VMEM)] * NY,
        out_shape=[piece] * NY,
        compiler_params=pltpu.CompilerParams(vmem_limit_bytes=VMEM),
        cost_estimate=pl.CostEstimate(flops=0, bytes_accessed=8 * keys.size, transcendentals=0),
    )(where, keys, values)


def pool_kernel(rows_ref, out_ref):
    count, rows = out_ref.shape[0], rows_ref.shape[0]
    j = lax.broadcasted_iota(jnp.int32, (count, rows), 0)
    r = lax.broadcasted_iota(jnp.int32, (count, rows), 1)
    inside = ((r <= 9 * j) & (r >= 9 * j - 8)).astype(jnp.bfloat16)
    total = jnp.dot(inside, rows_ref[...], preferred_element_type=jnp.float32)
    whole = lax.broadcasted_iota(jnp.int32, total.shape, 0) > 0
    out_ref[...] = jnp.where(whole, total / 9.0, total).astype(out_ref.dtype)


def pool(rows):
    count, width = rows.shape[0] // 9, rows.shape[1]
    return pl.pallas_call(
        pool_kernel,
        out_shape=jax.ShapeDtypeStruct((count, width), jnp.bfloat16),
        compiler_params=pltpu.CompilerParams(vmem_limit_bytes=VMEM),
        cost_estimate=pl.CostEstimate(
            flops=2 * count * rows.size, bytes_accessed=2 * rows.size + 2 * count * width, transcendentals=0
        ),
    )(rows)


def attend_kernel(n_kv, first, where_ref, *refs):
    q_refs, refs = refs[:NY], refs[NY:]
    kv_refs, refs = refs[:n_kv], refs[n_kv:]
    out_refs, (qs, ks, vs, ss) = refs[:NY], refs[NY:]
    y, z, xl = where_ref[0], where_ref[1], where_ref[2]
    rows, keys = qs.shape[1], ks.shape[1]
    ones = jnp.ones((keys, HEAD), jnp.bfloat16)
    base = (z * NX + xl) * rows
    for h in range(out_refs[0].shape[1] // HEAD):
        for d in range(NY):
            g = lax.rem(y + NY - d, NY)
            if d == 0:
                own = pl.ds(pl.multiple_of((y * GROUP + first + h) * HEAD, HEAD), HEAD)
                qs[g] = q_refs[d][:, own]
            else:
                qs[g] = q_refs[d][:, (first + h) * HEAD : (first + h + 1) * HEAD]
            for n, (shift, slots) in enumerate(KV_ORDER):
                zz = lax.rem(z + shift, NZ)
                at_head = first + h if kv_refs[n].shape[-1] == GROUP * HEAD else h
                column = slice(at_head * HEAD, at_head * HEAD + HEAD)
                for at, slot in enumerate(slots):
                    xx = xl if slot == 0 else 1 - xl
                    place = pl.ds(pl.multiple_of((zz * NX + xx) * 32, 32), 32)
                    ks[g, place, :] = kv_refs[n][d, 0, at * 32 : at * 32 + 32, column]
                    vs[g, place, :] = kv_refs[n][d, 1, at * 32 : at * 32 + 32, column]
        tops = [None] * NY
        for k in range(NY):
            q = qs[k:].reshape((NY - k) * rows, HEAD)
            s = lax.dot_general(q, ks[k], (((1,), (1,)), ((), ())), preferred_element_type=jnp.float32)
            for g in range(k, NY):
                part = s[(g - k) * rows : (g - k + 1) * rows]
                if k == g:
                    col = lax.broadcasted_iota(jnp.int32, part.shape, 1)
                    row = lax.broadcasted_iota(jnp.int32, part.shape, 0)
                    part = jnp.where(9 * col - row <= base, part, -1e30)
                ss[g * (g + 1) // 2 + k] = part
                here = jnp.max(part, axis=-1, keepdims=True)
                tops[g] = here if k == 0 else jnp.maximum(tops[g], here)
        sums = [jnp.zeros((rows, 2 * HEAD), jnp.float32) for _ in range(NY)]
        for k in range(NY):
            values = jnp.concatenate([vs[k], ones], axis=1)
            for g in range(k, NY):
                p = jnp.exp2((ss[g * (g + 1) // 2 + k] - tops[g]) * SCALE)
                sums[g] += jnp.dot(p.astype(jnp.bfloat16), values, preferred_element_type=jnp.float32)
        for g in range(NY):
            qs[g] = (sums[g][:, :HEAD] / sums[g][:, HEAD:]).astype(jnp.bfloat16)
        for d in range(NY):
            out_refs[d][:, h * HEAD : h * HEAD + HEAD] = qs[lax.rem(y + NY - d, NY)]


KV_ORDER = (
    (0, (0, 1)), (7, (0, 1)), (1, (0, 1)), (6, (0, 1)), (2, (0, 1)), (5, (0, 1)), (3, (0, 1)), (4, (0,)), (4, (1,)),
)


def attend(where, query, q_slots, arrivals, first, count):
    rows = query.shape[0]
    keys = NZ * NX * 32
    pairs = NY * (NY + 1) // 2 * rows * keys * count
    n_in = NY + len(arrivals)
    return pl.pallas_call(
        functools.partial(attend_kernel, len(arrivals), first),
        in_specs=[pl.BlockSpec(memory_space=pltpu.SMEM)] + [pl.BlockSpec(memory_space=pltpu.VMEM)] * n_in,
        out_specs=[pl.BlockSpec(memory_space=pltpu.VMEM)] * NY,
        out_shape=[jax.ShapeDtypeStruct((rows, count * HEAD), jnp.bfloat16)] * NY,
        scratch_shapes=[
            pltpu.VMEM((NY, rows, HEAD), jnp.bfloat16),
            pltpu.VMEM((NY, keys, HEAD), jnp.bfloat16),
            pltpu.VMEM((NY, keys, HEAD), jnp.bfloat16),
            pltpu.VMEM((NY * (NY + 1) // 2, rows, keys), jnp.float32),
        ],
        compiler_params=pltpu.CompilerParams(vmem_limit_bytes=VMEM),
        cost_estimate=pl.CostEstimate(
            flops=6 * pairs * HEAD, bytes_accessed=4 * NY * keys * HEAD * count, transcendentals=pairs
        ),
    )(where, query, *q_slots, *arrivals)


def base_kernel(mirrored_ref, short_ref, out_ref):
    rows, count = out_ref.shape[0], short_ref.shape[0]
    i = lax.broadcasted_iota(jnp.int32, (rows, count), 0)
    j = lax.broadcasted_iota(jnp.int32, (rows, count), 1)
    spread = ((i >= 9 * j) & (i < 9 * j + 9)).astype(jnp.bfloat16)
    total = jnp.dot(spread, short_ref[...], preferred_element_type=jnp.float32)
    out_ref[...] = mirrored_ref[...].astype(jnp.float32) + total


def base(mirrored, short_rows):
    return pl.pallas_call(
        base_kernel,
        in_specs=[pl.BlockSpec(memory_space=pltpu.VMEM)] * 2,
        out_specs=pl.BlockSpec(memory_space=pltpu.VMEM),
        out_shape=jax.ShapeDtypeStruct(mirrored.shape, jnp.float32),
        compiler_params=pltpu.CompilerParams(vmem_limit_bytes=VMEM),
        cost_estimate=pl.CostEstimate(
            flops=2 * short_rows.shape[0] * mirrored.size, bytes_accessed=6 * mirrored.size, transcendentals=0
        ),
    )(mirrored, short_rows)


def finish_kernel(where_ref, base_ref, pooled_ref, rim_ref, *refs):
    o_refs, (out_ref, bottle_ref, total, pooled, sems) = refs[:-5], refs[-5:]
    y, part = where_ref[0], GROUP * HEAD
    rows = pooled_ref[...].astype(jnp.float32)
    rim = jnp.sum(rim_ref[...].astype(jnp.float32), axis=0, keepdims=True)
    top = lax.broadcasted_iota(jnp.int32, rows.shape, 0) == 0
    pooled[...] = jnp.where(top, (rows + rim) / 9.0, rows).astype(pooled.dtype)
    copies = [pltpu.make_async_copy(pooled, bottle_ref, sems.at[NY])]
    copies[0].start()
    for d in range(NY):
        g = lax.rem(y + d, NY)
        for n, (first, heads) in enumerate(PHASES):
            columns = pl.ds(pl.multiple_of((g * GROUP + first) * HEAD, HEAD), heads * HEAD)
            summed = base_ref[:, columns] + o_refs[n * NY + d][...].astype(jnp.float32)
            total[:, columns] = summed.astype(out_ref.dtype)
        columns = pl.ds(pl.multiple_of(g * part, part), part)
        copies.append(pltpu.make_async_copy(total.at[:, columns], out_ref.at[:, columns], sems.at[d]))
        copies[-1].start()
    for copy in copies:
        copy.wait()


def finish(where, total, pooled, rim, o_slots):
    in_specs = [pl.BlockSpec(memory_space=pltpu.SMEM)]
    in_specs += [pl.BlockSpec(memory_space=pltpu.VMEM)] * (3 + len(o_slots))
    return pl.pallas_call(
        finish_kernel,
        in_specs=in_specs,
        out_specs=[pl.BlockSpec(memory_space=pltpu.HBM)] * 2,
        out_shape=[
            jax.ShapeDtypeStruct(total.shape, jnp.bfloat16),
            jax.ShapeDtypeStruct(pooled.shape, jnp.bfloat16),
        ],
        scratch_shapes=[
            pltpu.VMEM(total.shape, jnp.bfloat16),
            pltpu.VMEM(pooled.shape, jnp.bfloat16),
            pltpu.SemaphoreType.DMA((NY + 1,)),
        ],
        compiler_params=pltpu.CompilerParams(vmem_limit_bytes=VMEM),
        cost_estimate=pl.CostEstimate(flops=total.size, bytes_accessed=8 * total.size, transcendentals=0),
    )(where, total, pooled, rim, *o_slots)


def ring_step(step, ahead, back):
    if step == 4:
        half = ahead.shape[2] // 2
        ahead, back = ahead[:, :, :half], back[:, :, half:]
    return [move(ahead, dz=1), move(back, dz=-1)]


def ring_steps(arrived, steps):
    for step in steps:
        arrived = arrived + ring_step(step, *(arrived[-2:] if step > 1 else arrived * 2))
    return arrived


def body(stream, query, short_key, short_value, short_out):
    stream_rows, query_rows = stream[0], query[0]
    rows = stream_rows.shape[0]
    seq = lax.axis_index("seq")
    y, z, xl = seq // (NZ * NX), seq // NX % NZ, seq % NX
    where = jnp.stack([y, z, xl]).astype(jnp.int32)
    part = GROUP * HEAD

    pieces = pack(where, short_key[0], short_value[0])
    own = [pieces[0]] + [move(pieces[d], dy=d) for d in range(1, NY)]
    mine = jnp.stack(own)
    other = [move(after(pieces[d], own[1]), dy=d, dx=1) for d in range(NY)]
    others = jnp.stack(other)
    block = jnp.concatenate([mine, others], axis=2)

    query_late = after(query_rows, block)
    q_slots = [
        move(lax.dynamic_slice_in_dim(query_late, (y + d) % NY * part, part, 1), dy=d)
        for d in range(1, NY)
    ]
    mirrored = section_shift(after(stream_rows, block), 2)

    def attended(phase, arrivals):
        results = attend(where, query_rows, q_slots, arrivals, *PHASES[phase])
        return results[0], [results[0]] + [move(results[d], dy=-d) for d in range(1, NY)]

    first_in = [jnp.concatenate(pair, axis=2) for pair in zip(ring_step(1, mine, mine), ring_step(1, others, others))]
    first_in = list(lax.optimization_barrier(tuple(first_in)))
    both = [block, *[after(v, q_slots[0]) for v in first_in]]
    both = ring_steps(both, [2])
    ends = [after(v, q_slots[2]) for v in both[-2:]]
    a, b = [[v[..., first * HEAD : (first + heads) * HEAD] for v in ends] for first, heads in PHASES]
    a = both + ring_steps(a, [3, 4])[2:]
    b = both + ring_steps(b, [3])[2:]
    done, a_slots = attended(0, a)
    b = ring_steps([*b[:-2], *[after(v, done) for v in b[-2:]]], [4])
    done, b_slots = attended(1, [after(b[0], mirrored), *b[1:]])
    o_slots = a_slots + b_slots
    pooled = pool(stream_rows)
    bottleneck = section_shift(after(pooled, done, *a_slots[1:]), 1)
    rim = next_rows(after(stream_rows[rows - 8 :], done, *a_slots[1:]))
    total = base(after(mirrored, done), short_out[0])
    output, bottleneck = finish(where, total, bottleneck, rim, o_slots)
    return (output[None], bottleneck[None])


def solution(mesh):
    spec = P("section", "seq", None)
    return jax.shard_map(
        body, mesh=mesh, in_specs=(spec,) * 5, out_specs=(spec, spec), check_vma=False
    )
```

```python
import functools
import math

import jax
import jax.numpy as jnp
from jax import lax
from jax.experimental import pallas as pl
from jax.experimental.pallas import tpu as pltpu
from jax.sharding import PartitionSpec as P

HEADS = 20
HEAD = 128
NY, NZ, NX = 4, 8, 2
GROUP = HEADS // NY
PHASES = ((0, 3), (3, 2))
SCALE = math.log2(math.e) / math.sqrt(HEAD)
VMEM = 15 * 1024 * 1024


def seq_pairs(dy, dz, dx):
    pairs = []
    for y in range(NY):
        for z in range(NZ):
            for x in range(NX):
                to = (((y + dy) % NY) * NZ + (z + dz) % NZ) * NX + (x + dx) % NX
                pairs.append(((y * NZ + z) * NX + x, to))
    return pairs


def move(block, dy=0, dz=0, dx=0):
    return lax.ppermute(block, "seq", seq_pairs(dy, dz, dx))


def section_shift(block, by):
    count = lax.axis_size("section")
    return lax.ppermute(block, "section", [(i, (i + by) % count) for i in range(count)])


def next_rows(block):
    sections, count = lax.axis_size("section"), lax.axis_size("seq")
    pairs = [
        (s * count + i, (s + 1) % sections * count + i + 1) for s in range(sections) for i in range(count - 1)
    ]
    return lax.ppermute(block, ("section", "seq"), pairs)


def after(value, *others):
    return lax.optimization_barrier((value,) + others)[0]


def pack_kernel(where_ref, key_ref, value_ref, *out_refs):
    part = GROUP * HEAD
    for d in range(NY):
        group = lax.rem(where_ref[0] + d, NY)
        columns = pl.ds(pl.multiple_of(group * part, part), part)
        out_refs[d][0] = key_ref[:, columns]
        out_refs[d][1] = value_ref[:, columns]


def pack(where, keys, values):
    piece = jax.ShapeDtypeStruct((2, keys.shape[0], GROUP * HEAD), jnp.bfloat16)
    return pl.pallas_call(
        pack_kernel,
        in_specs=[pl.BlockSpec(memory_space=pltpu.SMEM)] + [pl.BlockSpec(memory_space=pltpu.VMEM)] * 2,
        out_specs=[pl.BlockSpec(memory_space=pltpu.VMEM)] * NY,
        out_shape=[piece] * NY,
        compiler_params=pltpu.CompilerParams(vmem_limit_bytes=VMEM),
        cost_estimate=pl.CostEstimate(flops=0, bytes_accessed=8 * keys.size, transcendentals=0),
    )(where, keys, values)


def pool_kernel(rows_ref, out_ref):
    count, rows = out_ref.shape[0], rows_ref.shape[0]
    j = lax.broadcasted_iota(jnp.int32, (count, rows), 0)
    r = lax.broadcasted_iota(jnp.int32, (count, rows), 1)
    inside = ((r <= 9 * j) & (r >= 9 * j - 8)).astype(jnp.bfloat16)
    total = jnp.dot(inside, rows_ref[...], preferred_element_type=jnp.float32)
    whole = lax.broadcasted_iota(jnp.int32, total.shape, 0) > 0
    out_ref[...] = jnp.where(whole, total / 9.0, total).astype(out_ref.dtype)


def pool(rows):
    count, width = rows.shape[0] // 9, rows.shape[1]
    return pl.pallas_call(
        pool_kernel,
        out_shape=jax.ShapeDtypeStruct((count, width), jnp.bfloat16),
        compiler_params=pltpu.CompilerParams(vmem_limit_bytes=VMEM),
        cost_estimate=pl.CostEstimate(
            flops=2 * count * rows.size, bytes_accessed=2 * rows.size + 2 * count * width, transcendentals=0
        ),
    )(rows)


def attend_kernel(n_kv, first, where_ref, *refs):
    q_refs, refs = refs[:NY], refs[NY:]
    kv_refs, refs = refs[:n_kv], refs[n_kv:]
    out_refs, (qs, ks, vs, ss) = refs[:NY], refs[NY:]
    y, z, xl = where_ref[0], where_ref[1], where_ref[2]
    rows, keys = qs.shape[1], ks.shape[1]
    ones = jnp.ones((keys, HEAD), jnp.bfloat16)
    base = (z * NX + xl) * rows
    for h in range(out_refs[0].shape[1] // HEAD):
        for d in range(NY):
            g = lax.rem(y + NY - d, NY)
            if d == 0:
                own = pl.ds(pl.multiple_of((y * GROUP + first + h) * HEAD, HEAD), HEAD)
                qs[g] = q_refs[d][:, own]
            else:
                qs[g] = q_refs[d][:, (first + h) * HEAD : (first + h + 1) * HEAD]
            for n, (shift, slots) in enumerate(KV_ORDER):
                zz = lax.rem(z + shift, NZ)
                at_head = first + h if kv_refs[n].shape[-1] == GROUP * HEAD else h
                column = slice(at_head * HEAD, at_head * HEAD + HEAD)
                for at, slot in enumerate(slots):
                    xx = xl if slot == 0 else 1 - xl
                    place = pl.ds(pl.multiple_of((zz * NX + xx) * 32, 32), 32)
                    ks[g, place, :] = kv_refs[n][d, 0, at * 32 : at * 32 + 32, column]
                    vs[g, place, :] = kv_refs[n][d, 1, at * 32 : at * 32 + 32, column]
        tops = [None] * NY
        for k in range(NY):
            q = qs[k:].reshape((NY - k) * rows, HEAD)
            s = lax.dot_general(q, ks[k], (((1,), (1,)), ((), ())), preferred_element_type=jnp.float32)
            for g in range(k, NY):
                part = s[(g - k) * rows : (g - k + 1) * rows]
                if k == g:
                    col = lax.broadcasted_iota(jnp.int32, part.shape, 1)
                    row = lax.broadcasted_iota(jnp.int32, part.shape, 0)
                    part = jnp.where(9 * col - row <= base, part, -1e30)
                ss[g * (g + 1) // 2 + k] = part
                here = jnp.max(part, axis=-1, keepdims=True)
                tops[g] = here if k == 0 else jnp.maximum(tops[g], here)
        sums = [jnp.zeros((rows, 2 * HEAD), jnp.float32) for _ in range(NY)]
        for k in range(NY):
            values = jnp.concatenate([vs[k], ones], axis=1)
            for g in range(k, NY):
                p = jnp.exp2((ss[g * (g + 1) // 2 + k] - tops[g]) * SCALE)
                sums[g] += jnp.dot(p.astype(jnp.bfloat16), values, preferred_element_type=jnp.float32)
        for g in range(NY):
            qs[g] = (sums[g][:, :HEAD] / sums[g][:, HEAD:]).astype(jnp.bfloat16)
        for d in range(NY):
            out_refs[d][:, h * HEAD : h * HEAD + HEAD] = qs[lax.rem(y + NY - d, NY)]


KV_ORDER = (
    (0, (0, 1)), (7, (0, 1)), (1, (0, 1)), (6, (0, 1)), (2, (0, 1)), (5, (0, 1)), (3, (0, 1)), (4, (0,)), (4, (1,)),
)


def attend(where, query, q_slots, arrivals, first, count):
    rows = query.shape[0]
    keys = NZ * NX * 32
    pairs = NY * (NY + 1) // 2 * rows * keys * count
    n_in = NY + len(arrivals)
    return pl.pallas_call(
        functools.partial(attend_kernel, len(arrivals), first),
        in_specs=[pl.BlockSpec(memory_space=pltpu.SMEM)] + [pl.BlockSpec(memory_space=pltpu.VMEM)] * n_in,
        out_specs=[pl.BlockSpec(memory_space=pltpu.VMEM)] * NY,
        out_shape=[jax.ShapeDtypeStruct((rows, count * HEAD), jnp.bfloat16)] * NY,
        scratch_shapes=[
            pltpu.VMEM((NY, rows, HEAD), jnp.bfloat16),
            pltpu.VMEM((NY, keys, HEAD), jnp.bfloat16),
            pltpu.VMEM((NY, keys, HEAD), jnp.bfloat16),
            pltpu.VMEM((NY * (NY + 1) // 2, rows, keys), jnp.float32),
        ],
        compiler_params=pltpu.CompilerParams(vmem_limit_bytes=VMEM),
        cost_estimate=pl.CostEstimate(
            flops=6 * pairs * HEAD, bytes_accessed=4 * NY * keys * HEAD * count, transcendentals=pairs
        ),
    )(where, query, *q_slots, *arrivals)


def base_kernel(mirrored_ref, short_ref, out_ref):
    rows, count = out_ref.shape[0], short_ref.shape[0]
    i = lax.broadcasted_iota(jnp.int32, (rows, count), 0)
    j = lax.broadcasted_iota(jnp.int32, (rows, count), 1)
    spread = ((i >= 9 * j) & (i < 9 * j + 9)).astype(jnp.bfloat16)
    total = jnp.dot(spread, short_ref[...], preferred_element_type=jnp.float32)
    out_ref[...] = mirrored_ref[...].astype(jnp.float32) + total


def base(mirrored, short_rows):
    return pl.pallas_call(
        base_kernel,
        in_specs=[pl.BlockSpec(memory_space=pltpu.VMEM)] * 2,
        out_specs=pl.BlockSpec(memory_space=pltpu.VMEM),
        out_shape=jax.ShapeDtypeStruct(mirrored.shape, jnp.float32),
        compiler_params=pltpu.CompilerParams(vmem_limit_bytes=VMEM),
        cost_estimate=pl.CostEstimate(
            flops=2 * short_rows.shape[0] * mirrored.size, bytes_accessed=6 * mirrored.size, transcendentals=0
        ),
    )(mirrored, short_rows)


def finish_kernel(where_ref, base_ref, pooled_ref, rim_ref, *refs):
    o_refs, (out_ref, bottle_ref, total, pooled, sems) = refs[:-5], refs[-5:]
    y, part = where_ref[0], GROUP * HEAD
    rows = pooled_ref[...].astype(jnp.float32)
    rim = jnp.sum(rim_ref[...].astype(jnp.float32), axis=0, keepdims=True)
    top = lax.broadcasted_iota(jnp.int32, rows.shape, 0) == 0
    pooled[...] = jnp.where(top, (rows + rim) / 9.0, rows).astype(pooled.dtype)
    copies = [pltpu.make_async_copy(pooled, bottle_ref, sems.at[NY])]
    copies[0].start()
    for d in range(NY):
        g = lax.rem(y + d, NY)
        for n, (first, heads) in enumerate(PHASES):
            columns = pl.ds(pl.multiple_of((g * GROUP + first) * HEAD, HEAD), heads * HEAD)
            summed = base_ref[:, columns] + o_refs[n * NY + d][...].astype(jnp.float32)
            total[:, columns] = summed.astype(out_ref.dtype)
        columns = pl.ds(pl.multiple_of(g * part, part), part)
        copies.append(pltpu.make_async_copy(total.at[:, columns], out_ref.at[:, columns], sems.at[d]))
        copies[-1].start()
    for copy in copies:
        copy.wait()


def finish(where, total, pooled, rim, o_slots):
    in_specs = [pl.BlockSpec(memory_space=pltpu.SMEM)]
    in_specs += [pl.BlockSpec(memory_space=pltpu.VMEM)] * (3 + len(o_slots))
    return pl.pallas_call(
        finish_kernel,
        in_specs=in_specs,
        out_specs=[pl.BlockSpec(memory_space=pltpu.HBM)] * 2,
        out_shape=[
            jax.ShapeDtypeStruct(total.shape, jnp.bfloat16),
            jax.ShapeDtypeStruct(pooled.shape, jnp.bfloat16),
        ],
        scratch_shapes=[
            pltpu.VMEM(total.shape, jnp.bfloat16),
            pltpu.VMEM(pooled.shape, jnp.bfloat16),
            pltpu.SemaphoreType.DMA((NY + 1,)),
        ],
        compiler_params=pltpu.CompilerParams(vmem_limit_bytes=VMEM),
        cost_estimate=pl.CostEstimate(flops=total.size, bytes_accessed=8 * total.size, transcendentals=0),
    )(where, total, pooled, rim, *o_slots)


def ring_step(step, ahead, back):
    if step == 4:
        half = ahead.shape[2] // 2
        ahead, back = ahead[:, :, :half], back[:, :, half:]
    return [move(ahead, dz=1), move(back, dz=-1)]


def ring_steps(arrived, steps):
    for step in steps:
        arrived = arrived + ring_step(step, *(arrived[-2:] if step > 1 else arrived * 2))
    return arrived


def body(stream, query, short_key, short_value, short_out):
    stream_rows, query_rows = stream[0], query[0]
    rows = stream_rows.shape[0]
    seq = lax.axis_index("seq")
    y, z, xl = seq // (NZ * NX), seq // NX % NZ, seq % NX
    where = jnp.stack([y, z, xl]).astype(jnp.int32)
    part = GROUP * HEAD

    pieces = pack(where, short_key[0], short_value[0])
    own = [pieces[0]] + [move(pieces[d], dy=d) for d in range(1, NY)]
    mine = jnp.stack(own)
    other = [move(after(pieces[d], own[1]), dy=d, dx=1) for d in range(NY)]
    others = jnp.stack(other)
    block = jnp.concatenate([mine, others], axis=2)

    query_late = after(query_rows, block)
    q_slots = [
        move(lax.dynamic_slice_in_dim(query_late, (y + d) % NY * part, part, 1), dy=d)
        for d in range(1, NY)
    ]
    mirrored = section_shift(after(stream_rows, block), 2)

    def attended(phase, arrivals, *needed):
        results = attend(where, query_rows, q_slots, arrivals, *PHASES[phase])
        sent = [move(after(results[d], *needed) if needed else results[d], dy=-d) for d in range(1, NY)]
        return results[0], [results[0]] + sent

    first_in = [jnp.concatenate(pair, axis=2) for pair in zip(ring_step(1, mine, mine), ring_step(1, others, others))]
    first_in = list(lax.optimization_barrier(tuple(first_in)))
    both = [block, *[after(v, q_slots[0]) for v in first_in]]
    both = ring_steps(both, [2])
    ends = [after(v, q_slots[2]) for v in both[-2:]]
    a, b = [[v[..., first * HEAD : (first + heads) * HEAD] for v in ends] for first, heads in PHASES]
    a = both + ring_steps(a, [3, 4])[2:]
    b = both + ring_steps(b, [3])[2:]
    done, a_slots = attended(0, a)
    b = ring_steps([*b[:-2], *[after(v, done) for v in b[-2:]]], [4])
    bottleneck = section_shift(after(pool(stream_rows), done, mirrored), 1)
    done, b_slots = attended(1, [after(b[0], mirrored), *b[1:]], bottleneck)
    o_slots = a_slots + b_slots
    rim = next_rows(after(stream_rows[rows - 8 :], done, *a_slots[1:]))
    total = base(after(mirrored, done), short_out[0])
    output, bottleneck = finish(where, total, bottleneck, rim, o_slots)
    return (output[None], bottleneck[None])


def solution(mesh):
    spec = P("section", "seq", None)
    return jax.shard_map(
        body, mesh=mesh, in_specs=(spec,) * 5, out_specs=(spec, spec), check_vma=False
    )
```
